256 devices in a mesh: section: 2 (over y_lo), req: 16 (over x, y_hi, core), tp: 8 (over z).
Axes of the slice: x: 4, y: 4 (y_hi: 2, y_lo: 2; y = y_hi * 2 + y_lo), z: 8, core: 2. Of those that a mesh axis runs over, the one named last changes fastest.
Arguments:
- draft_rows: bfloat16 [1024, 8192], P('tp', 'req'), may hold values from -4 to 4
- norm_gain: bfloat16 [2, 8192], P('section', 'req'), may hold values from 0.099609375 to 1.8984375
- w_query: bfloat16 [2, 8192, 8192], P('section', 'req', 'tp'), may hold values from -0.0625 to 0.0625
- w_keyval: bfloat16 [2, 2, 8192, 1024], P('section', None, 'req', 'tp'), may hold values from -0.0625 to 0.0625
- w_out: bfloat16 [2, 8192, 8192], P('section', 'tp', 'req'), may hold values from -0.0625 to 0.0625
- kv_cache: bfloat16 [2, 16, 2, 4096, 1024], P('section', 'req', None, None, 'tp'), may hold values from -360 to 360
- tree_counts: int32 [16], P('req'), may hold values from 16 to 64, as said below
- cache_lengths: int32 [16], P('req'), may hold values from 512 to 4096, as said below
- tree_parents: int32 [16, 64], P('req'), may hold values from 0 to 62, as said below
Outputs:
- layer_outputs: bfloat16 [2, 1024, 8192], P('section', 'tp', 'req')
The draws below stay inside these ranges and needn't reach their ends.
Inputs may be any that keep to these rules, and one draw needn't show every extreme that they name: Live rows of request r are its slots 0 to tree_counts[r] - 1; some request has all 64 live. Positions 0 to cache_lengths[r] - 1 are in use; some request uses all 4096. `tree_parents`: the parent of slot t > 0 is a slot below t; slot 0 names itself.
All inputs are finite; a program needn't handle non-finite values.
Results may differ from the reference program's by a relative error of at most 0.03.
Values may be sent and summed in bfloat16 or wider, within the bound.
A program may use at most 64 MiB of HBM per device.

```python
import jax
import jax.numpy as jnp
from jax import lax

D = 8192
HEADS = 64
KV_HEADS = 8
HEAD_DIM = 128
TREE = 64
CACHE = 4096
LAYERS = 2
REQUESTS = 16
ROWS = 1024


def draw_draft_rows(key, part):
    key = jax.random.fold_in(key, 11)
    first, second, third = jax.random.split(key, 3)
    ramp = jnp.arange(D, dtype=jnp.float32) / max(D - 1, 1)
    base = jax.random.truncated_normal(first, -4.0, 4.0, (ROWS, D), jnp.float32)
    row_scale = 10.0 ** jax.random.uniform(second, (ROWS, 1), jnp.float32)
    col_scale = 10.0 ** jax.random.uniform(third, (1, D), jnp.float32) * (3.0 ** ramp)[None, :]
    return (base * row_scale * col_scale / 300.0).astype(jnp.bfloat16)


def draw_kv_cache(key, part):
    key = jax.random.fold_in(key, 5)
    first = jax.random.fold_in(key, 0)
    shape = (LAYERS, REQUESTS, 2, CACHE, KV_HEADS * HEAD_DIM)
    values = jax.random.truncated_normal(first, -4.0, 4.0, shape, jnp.float32)
    return values.astype(jnp.bfloat16)


def draw_tree_counts(key, part):
    key = jax.random.fold_in(key, 7)
    first, second = jax.random.split(key, 2)
    counts = jax.random.randint(first, (REQUESTS,), TREE // 4, TREE + 1)
    chosen = jax.random.randint(second, (), 0, REQUESTS)
    return jnp.where(jnp.arange(REQUESTS, dtype=jnp.int32) == chosen, TREE, counts).astype(jnp.int32)


def draw_cache_lengths(key, part):
    key = jax.random.fold_in(key, 9)
    first, second = jax.random.split(key, 2)
    lengths = jax.random.randint(first, (REQUESTS,), CACHE // 8, CACHE + 1)
    chosen = jax.random.randint(second, (), 0, REQUESTS)
    return jnp.where(jnp.arange(REQUESTS, dtype=jnp.int32) == chosen, CACHE, lengths).astype(jnp.int32)


def draw_tree_parents(key, part):
    key = jax.random.fold_in(key, 13)
    slots = jnp.arange(TREE, dtype=jnp.int32)
    upper = jnp.broadcast_to(jnp.maximum(slots, 1)[None, :], (REQUESTS, TREE))
    parents = jax.random.randint(key, (REQUESTS, TREE), 0, upper)
    parents = jnp.where(slots[None, :] == TREE - 1, TREE - 2, parents)
    return parents.astype(jnp.int32)


def level_of(key, extent, shards, least, high):
    level = 1.0
    for dim, blocks in shards:
        heights = jax.random.uniform(jax.random.fold_in(jax.random.fold_in(key, 6), dim), (blocks,), jnp.float32, least / len(shards), high / len(shards))
        level = level * jnp.repeat(jnp.exp(heights), extent[dim] // blocks).reshape((-1,) + (1,) * (len(extent) - 1 - dim))
    return level


def gaussian(rng, shape, width, limit, cuts=(), kind=jnp.bfloat16):
    factor_of = level_of(rng, shape, cuts, -0.22, 0.18) if cuts else 1.0
    array = jax.random.normal(rng, shape, jnp.float32) * width * factor_of
    return jnp.minimum(jnp.maximum(array, -limit), limit).astype(kind)


def setup_inputs(seed: int = 0) -> dict:
    arg_keys = jax.random.split(jax.random.key(seed), 10)
    return {
        "draft_rows": draw_draft_rows(jax.random.fold_in(arg_keys[9], 71), 0),
        "norm_gain": jnp.clip(1.0 + 0.18 * jax.random.normal(arg_keys[1], (LAYERS, D), jnp.float32), 0.099609375, 1.8984375).astype(jnp.bfloat16),
        "w_query": gaussian(arg_keys[2], (LAYERS, D, HEADS * HEAD_DIM), D ** -0.5, 0.0625, ((0, 2), (1, 16), (2, 8))),
        "w_keyval": gaussian(arg_keys[3], (LAYERS, 2, D, KV_HEADS * HEAD_DIM), D ** -0.5, 0.0625, ((0, 2), (2, 16), (3, 8))),
        "w_out": gaussian(arg_keys[4], (LAYERS, HEADS * HEAD_DIM, D), (HEADS * HEAD_DIM) ** -0.5, 0.0625, ((0, 2), (1, 8), (2, 16))),
        "kv_cache": draw_kv_cache(jax.random.fold_in(arg_keys[9], 71), 0),
        "tree_counts": draw_tree_counts(jax.random.fold_in(arg_keys[9], 71), 0),
        "cache_lengths": draw_cache_lengths(jax.random.fold_in(arg_keys[9], 71), 0),
        "tree_parents": draw_tree_parents(jax.random.fold_in(arg_keys[9], 71), 0),
    }


EPSILON = 1e-05

def ancestors(parents):
    indices = jnp.arange(TREE, dtype=jnp.int32)
    links = (parents[:, None] == indices[None, :]).astype(jnp.float32)
    reach = jnp.minimum(links + jnp.eye(TREE, dtype=jnp.float32), 1.0)
    for sweep in range(max(1, (TREE - 1).bit_length())):
        reach = jnp.minimum(jnp.dot(reach, reach, precision=lax.Precision.HIGHEST), 1.0)
    return reach

def attend(query, key_new, value_new, cache_keys, cache_values, length, reach):
    tree = query.shape[0]
    cache_len = cache_keys.shape[0]
    kv_count = cache_keys.shape[1] // HEAD_DIM
    group = query.shape[1] // cache_keys.shape[1]
    heads = query.reshape(tree, kv_count, group, HEAD_DIM).astype(jnp.float32)
    old_keys = cache_keys.reshape(cache_len, kv_count, HEAD_DIM).astype(jnp.float32)
    old_values = cache_values.reshape(cache_len, kv_count, HEAD_DIM).astype(jnp.float32)
    new_keys = key_new.reshape(tree, kv_count, HEAD_DIM).astype(jnp.float32)
    new_values = value_new.reshape(tree, kv_count, HEAD_DIM).astype(jnp.float32)
    factor = HEAD_DIM ** (-0.5)
    score_cache = jnp.einsum('tkgd,ckd->kgtc', heads, old_keys) * factor
    score_tree = jnp.einsum('tkgd,skd->kgts', heads, new_keys) * factor
    in_use = jnp.arange(cache_len, dtype=jnp.int32) < length
    score_cache = jnp.where(in_use, score_cache, -jnp.inf)
    score_tree = jnp.where(reach > 0.5, score_tree, -jnp.inf)
    top = jnp.maximum(lax.optimization_barrier(jnp.max(score_cache, axis=-1)), lax.optimization_barrier(jnp.max(score_tree, axis=-1)))
    weight_cache = jnp.exp(score_cache - top[..., None])
    weight_tree = jnp.exp(score_tree - top[..., None])
    total = lax.optimization_barrier(jnp.sum(weight_cache, axis=-1)) + lax.optimization_barrier(jnp.sum(weight_tree, axis=-1))
    rounded_cache = weight_cache.astype(jnp.bfloat16).astype(jnp.float32)
    rounded_tree = weight_tree.astype(jnp.bfloat16).astype(jnp.float32)
    mixed = jnp.einsum('kgtc,ckd->tkgd', rounded_cache, old_values)
    mixed = mixed + jnp.einsum('kgts,skd->tkgd', rounded_tree, new_values)
    mixed = mixed / jnp.transpose(total, (2, 0, 1))[..., None]
    return mixed.reshape(tree, kv_count * group * HEAD_DIM)

def layer(rows, gain, w_q, w_kv, w_o, cache, lengths, counts, parents):
    rows_wide = rows.astype(jnp.float32)
    squares = lax.optimization_barrier(jnp.sum(rows_wide * rows_wide, axis=1))
    inverse = lax.rsqrt(squares / D + EPSILON)
    scaled = (rows_wide * gain.astype(jnp.float32)).astype(jnp.bfloat16)
    query = (jnp.dot(scaled, w_q, preferred_element_type=jnp.float32) * inverse[:, None]).astype(jnp.bfloat16)
    keys_new = (jnp.dot(scaled, w_kv[0], preferred_element_type=jnp.float32) * inverse[:, None]).astype(jnp.bfloat16)
    values_new = (jnp.dot(scaled, w_kv[1], preferred_element_type=jnp.float32) * inverse[:, None]).astype(jnp.bfloat16)
    reach = jax.vmap(ancestors)(parents)
    query = query.reshape(REQUESTS, TREE, query.shape[1])
    keys_new = keys_new.reshape(REQUESTS, TREE, keys_new.shape[1])
    values_new = values_new.reshape(REQUESTS, TREE, values_new.shape[1])
    mixed = lax.map(lambda items: attend(*items), (query, keys_new, values_new, cache[:, 0], cache[:, 1], lengths, reach))
    live = (jnp.arange(TREE, dtype=jnp.int32)[None, :] < counts[:, None]).astype(jnp.float32)
    attended = (mixed * live[:, :, None]).reshape(ROWS, mixed.shape[2]).astype(jnp.bfloat16)
    return (jnp.dot(attended, w_o, preferred_element_type=jnp.float32) + rows_wide).astype(jnp.bfloat16)

def reference(draft_rows, norm_gain, w_query, w_keyval, w_out, kv_cache, tree_counts, cache_lengths, tree_parents):
    first = layer(draft_rows, norm_gain[0], w_query[0], w_keyval[0], w_out[0], kv_cache[0], cache_lengths, tree_counts, tree_parents)
    second = layer(first, norm_gain[1], w_query[1], w_keyval[1], w_out[1], kv_cache[1], cache_lengths, tree_counts, tree_parents)
    return jnp.stack([first, second])
```

```python
import functools

import jax
import jax.numpy as jnp
from jax import lax
from jax.experimental import pallas as pl
from jax.experimental.pallas import tpu as pltpu
from jax.sharding import PartitionSpec as P

MESH = pl.DeviceIdType.MESH
F32, BF16 = jnp.float32, jnp.bfloat16

D = 8192
HEAD_DIM = 128
TREE = 64
EPSILON = 1e-05

BATCHES = 4
SLOTS = TREE // BATCHES
OFFSET = 1
KEY_BLOCK = 1024
NX, NY, NZ = 4, 2, 8
CHIPS = NX * NY
OWN = 2
SCORE_SCALE = HEAD_DIM ** -0.5 * 1.4426950408889634
LOW = -1e30

ROWS1, ROWS2, ROWS_SIB, SUMS, SQUARES, HEADS, HEADS_SIB, OUT1, OUT2, HAND = range(10)


def dot(a, b):
    return jnp.dot(a, b, preferred_element_type=F32)


def dot_nt(a, b):
    return lax.dot_general(a, b, (((1,), (1,)), ((), ())), preferred_element_type=F32)


def kernel(
    draft, gain, w_query, w_keyval, w_out, cache, parents, counts, lengths, out,
    rows, gains, w_in, w_o, keys, values, values_t, part, sums, sq_send, sq_recv,
    keys_new, values_new, reach, scores, heads, outp, out1, merged, out2, handed,
    send, recv, local, sib_send, sib_recv,
):
    T = SLOTS
    sec = lax.axis_index("section")
    req = lax.axis_index("req")
    z = lax.axis_index("tp")
    chip, core = req // 2, req % 2
    x, y = chip // NY, chip % NY
    key_blocks, key_block = scores.shape[0], scores.shape[1]
    lanes = scores.shape[2]

    def along(by):
        return (sec, req, (z + by + NZ) % NZ)

    sibling = (sec, chip * 2 + (1 - core), z)

    def planar(dx, dy, dc):
        to_chip = ((x + dx) % NX) * NY + (y + dy) % NY
        to_core = (core + dc) % 2
        return to_chip, to_core, (sec, to_chip * 2 + to_core, z)

    other_section = (1 - sec, req, z)
    offsets = [(dx, dy) for dx in range(NX) for dy in range(NY)]
    near = (1, -1, 2, -2)

    def push(src, dst, phase, m, device):
        pltpu.make_async_remote_copy(
            src_ref=src, dst_ref=dst, send_sem=send.at[m, phase], recv_sem=recv.at[m, phase],
            device_id=device, device_id_type=MESH,
        ).start()

    def await_bytes(ref, sem):
        pltpu.make_async_copy(ref, ref, sem).wait()

    @pl.when(sec == 0)
    def _():
        for m in range(BATCHES):
            pltpu.make_async_copy(
                draft.at[:, pl.ds(m * T, T)], rows.at[m, core, OWN], recv.at[m, HAND]
            ).start()

    half = w_in.shape[2] - HEAD_DIM
    loads = [
        pltpu.make_async_copy(
            w_query.at[0, :, pl.ds(pl.multiple_of(core * half, 128), half)],
            w_in.at[core, :, pl.ds(0, half)], local.at[0]),
        pltpu.make_async_copy(
            w_keyval.at[0, core], w_in.at[core, :, pl.ds(half, HEAD_DIM)], local.at[1]),
        pltpu.make_async_copy(cache.at[0, 0, 1], values, local.at[2]),
        pltpu.make_async_copy(cache.at[0, 0, 0], keys, local.at[3]),
        pltpu.make_async_copy(w_out.at[0], w_o, local.at[4]),
    ]
    for load in loads:
        load.start()
    gains[core] = jnp.broadcast_to(gain[...].astype(F32), gains.shape[1:])

    barrier = pltpu.get_barrier_semaphore()
    partners = [along(by) for by in near] + [sibling, other_section]
    partners += [planar(dx, dy, dc)[2] for dx, dy in offsets if (dx, dy) != (0, 0) for dc in range(2)]
    for device in partners:
        pl.semaphore_signal(barrier, inc=1, device_id=device, device_id_type=MESH)
    pl.semaphore_wait(barrier, len(partners))

    def step_rows(m):
        await_bytes(rows.at[0, 0, 0], recv.at[m, HAND])
        for by in near:
            push(rows.at[m, core, OWN], rows.at[m, core, OWN - by], ROWS1, m, along(by))

    @pl.when(sec == 0)
    def _():
        def each(m, carry):
            step_rows(m)
            return carry
        lax.fori_loop(0, BATCHES, each, 0)

    to_sibling = [
        pltpu.make_async_remote_copy(
            src_ref=gains.at[core], dst_ref=gains.at[core], send_sem=sib_send.at[0], recv_sem=sib_recv.at[0],
            device_id=sibling, device_id_type=MESH),
        pltpu.make_async_remote_copy(
            src_ref=w_query.at[0, :, pl.ds(pl.multiple_of((1 - core) * half, 128), half)],
            dst_ref=w_in.at[core, :, pl.ds(0, half)], send_sem=sib_send.at[1], recv_sem=sib_recv.at[1],
            device_id=sibling, device_id_type=MESH),
        pltpu.make_async_remote_copy(
            src_ref=w_keyval.at[0, 1 - core], dst_ref=w_in.at[core, :, pl.ds(half, HEAD_DIM)],
            send_sem=sib_send.at[2], recv_sem=sib_recv.at[2], device_id=sibling, device_id_type=MESH),
    ]
    for copy in to_sibling:
        copy.start()

    row_index = lax.broadcasted_iota(jnp.int32, (TREE, TREE), 0)
    col_index = lax.broadcasted_iota(jnp.int32, (TREE, TREE), 1)
    closure = jnp.where((parents[...] == row_index) | (row_index == col_index), 1.0, 0.0)
    for _ in range(6):
        closure = jnp.minimum(dot(closure.astype(BF16), closure.astype(BF16)), 1.0)
    reach[...] = closure.astype(BF16)
    keys_new[...] = jnp.zeros_like(keys_new)
    values_new[...] = jnp.zeros_like(values_new)

    diagonal = lax.broadcasted_iota(jnp.int32, (HEAD_DIM, HEAD_DIM), 0) == lax.broadcasted_iota(
        jnp.int32, (HEAD_DIM, HEAD_DIM), 1)
    identity = jnp.where(diagonal, 1.0, 0.0).astype(BF16)
    loads[2].wait()

    def turn(b, carry):
        values_t[b] = dot_nt(identity, values[pl.ds(pl.multiple_of(b * key_block, key_block), key_block), :]).astype(BF16)
        return carry
    lax.fori_loop(0, key_blocks, turn, 0)
    loads[3].wait()
    loads[4].wait()
    loads[0].wait()
    loads[1].wait()
    for copy in to_sibling:
        copy.wait()

    length = lengths[0]
    count = counts[0]

    def step_pass(m):
        await_bytes(rows.at[0, 0, pl.ds(0, 4)], recv.at[m, ROWS1])
        push(rows.at[m, core, 0], rows.at[m, core, 7], ROWS2, m, along(1))
        push(rows.at[m, core, 4], rows.at[m, core, 5], ROWS2, m, along(-1))
        push(rows.at[m, core, 0, 0], rows.at[m, core, 6, 0], ROWS2, m, along(2))
        push(rows.at[m, core, 4, 1], rows.at[m, core, 6, 1], ROWS2, m, along(-2))
        push(rows.at[m, core, pl.ds(0, 5)], rows.at[m, core, pl.ds(0, 5)], ROWS_SIB, m, sibling)

    def step_last_rows(m):
        await_bytes(rows.at[0, 0, pl.ds(0, 3)], recv.at[m, ROWS2])
        push(rows.at[m, core, pl.ds(5, 3)], rows.at[m, core, pl.ds(5, 3)], ROWS_SIB, m, sibling)

    def step_project(m):
        await_bytes(rows.at[0, 0], recv.at[m, ROWS_SIB])
        total_sq = None
        total = None
        for s in range(2):
            block = rows[m, s].reshape(CHIPS * 2 * T, rows.shape[-1]).astype(F32)
            sq = jnp.sum(block * block, axis=1, keepdims=True)
            scaled = (block * gains[s, 0:1, :]).astype(BF16)
            product = dot(scaled, w_in[s])
            total = product if total is None else total + product
            total_sq = sq if total_sq is None else total_sq + sq
        part[m] = total.reshape(CHIPS, 2, T, total.shape[1]).astype(BF16)
        wide = jnp.broadcast_to(total_sq, (CHIPS * 2 * T, HEAD_DIM))
        lane = lax.broadcasted_iota(jnp.int32, wide.shape, 1)
        high = wide.astype(BF16)
        low = (wide - high.astype(F32)).astype(BF16)
        packed = jnp.where(lane == 0, high.astype(F32), jnp.where(lane == 1, low.astype(F32), 0.0))
        sq_send[m] = packed.reshape(CHIPS, 2, T, HEAD_DIM).astype(BF16)
        for dx, dy in offsets:
            for dc in range(2):
                if (dx, dy, dc) == (0, 0, 0):
                    continue
                to_chip, to_core, device = planar(dx, dy, dc)
                place = (to_chip - z + OWN + NZ) % NZ
                push(part.at[m, place, to_core], sums.at[m, dc * CHIPS + dx * NY + dy], SUMS, m, device)
                if dc == 0:
                    push(sq_send.at[m, place, to_core], sq_recv.at[m, dx * NY + dy], SQUARES, m, device)

    def step_attend(m):
        await_bytes(sums.at[0, pl.ds(0, 15)], recv.at[m, SUMS])
        await_bytes(sq_recv.at[0, pl.ds(0, 7)], recv.at[m, SQUARES])
        place = (chip - z + OWN + NZ) % NZ
        same = part[m, place, core].astype(F32)
        squares = sq_send[m, place, core].astype(F32)
        for k in range(1, CHIPS):
            same = same + sums[m, k].astype(F32)
            squares = squares + sq_recv[m, k].astype(F32)
        other = sums[m, CHIPS].astype(F32)
        for k in range(CHIPS + 1, 2 * CHIPS):
            other = other + sums[m, k].astype(F32)
        inverse = lax.rsqrt(jnp.sum(squares, axis=1, keepdims=True) / D + EPSILON)
        same = same * inverse
        other = other * inverse
        first = jnp.where(core == 0, same, other).astype(BF16)
        second = jnp.where(core == 0, other, same).astype(BF16)
        query = jnp.concatenate(
            [g[:, h * HEAD_DIM:(h + 1) * HEAD_DIM] for g in (first, second) for h in range(half // HEAD_DIM)], axis=0)
        slots = pl.ds(pl.multiple_of(m * T, T), T)
        keys_new[slots, :] = first[:, half:]
        values_new[slots, :] = second[:, half:]

        lane_slot = lax.broadcasted_iota(jnp.int32, (TREE, lanes), 1) % T + m * T
        pick = jnp.where(lax.broadcasted_iota(jnp.int32, (TREE, lanes), 0) == lane_slot, 1.0, 0.0).astype(BF16)
        reached = dot(reach[...], pick) > 0.5
        tree_scores = jnp.where(reached, dot_nt(keys_new[...], query), LOW)
        top = jnp.max(tree_scores, axis=0, keepdims=True)
        position = lax.broadcasted_iota(jnp.int32, (key_block, lanes), 0)
        for b in range(key_blocks):
            block = dot_nt(keys[b * key_block:(b + 1) * key_block, :], query)
            block = jnp.where(position < length - b * key_block, block, LOW)
            scores[b] = block
            top = jnp.maximum(top, jnp.max(block, axis=0, keepdims=True))
        weights = jnp.exp2((tree_scores - top) * SCORE_SCALE)
        total = jnp.sum(weights, axis=0, keepdims=True)
        values_new_t = dot_nt(identity, values_new[...]).astype(BF16)
        mixed = dot(values_new_t, weights.astype(BF16))
        for b in range(key_blocks):
            weights = jnp.exp2((scores[b] - top) * SCORE_SCALE)
            total = total + jnp.sum(weights, axis=0, keepdims=True)
            mixed = mixed + dot(values_t[b], weights.astype(BF16))
        live = lax.broadcasted_iota(jnp.int32, (1, lanes), 1) % T + m * T < count
        mixed = jnp.where(live, mixed / total, 0.0).T.astype(BF16)
        for h in range(lanes // T):
            heads[m, core, chip, :, h * HEAD_DIM:(h + 1) * HEAD_DIM] = mixed[h * T:(h + 1) * T, :]
        for dx, dy in offsets:
            if (dx, dy) != (0, 0):
                push(heads.at[m, core, chip], heads.at[m, core, chip], HEADS, m, planar(dx, dy, 0)[2])

    def step_heads(m):
        await_bytes(heads.at[0, 0, pl.ds(0, 7)], recv.at[m, HEADS])
        push(heads.at[m, core], heads.at[m, core], HEADS_SIB, m, sibling)

    def step_out(m):
        await_bytes(heads.at[0, 0], recv.at[m, HEADS_SIB])
        product = dot(heads[m].reshape(2 * CHIPS * T, heads.shape[-1]), w_o[...]).astype(BF16)
        product = product.reshape(2, CHIPS, T, product.shape[1])
        for i in range(2):
            outp[m, :, i] = product[i]
        push(outp.at[m, (z + 3) % NZ], out1.at[m, 0], OUT1, m, along(1))
        push(outp.at[m, (z + 5) % NZ], out1.at[m, 1], OUT1, m, along(-1))
        push(outp.at[m, (z + 4) % NZ, 0], out1.at[m, 2, 0], OUT1, m, along(2))
        push(outp.at[m, (z + 4) % NZ, 1], out1.at[m, 2, 1], OUT1, m, along(-2))
        push(outp.at[m, (z + 1) % NZ], out2.at[m, 2], OUT2, m, along(1))
        push(outp.at[m, (z + 7) % NZ], out2.at[m, 3], OUT2, m, along(-1))

    def step_merge(m):
        await_bytes(out1.at[0], recv.at[m, OUT1])
        for side, by in enumerate((2, -2)):
            both = outp[m, (z + by + NZ) % NZ].astype(F32) + out1[m, side].astype(F32)
            merged[m, side] = both.astype(BF16)
            merged[m, side, side] = (both[side] + out1[m, 2, side].astype(F32)).astype(BF16)
            push(merged.at[m, side], out2.at[m, side], OUT2, m, along(by))

    def step_finish(m):
        await_bytes(out2.at[0], recv.at[m, OUT2])
        total = outp[m, z].astype(F32)
        for k in range(4):
            total = total + out2[m, k].astype(F32)
        result = (total + rows[m, core, OWN].astype(F32)).astype(BF16)
        out[:, pl.ds(pl.multiple_of(m * T, T), T), :] = result

        @pl.when(sec == 0)
        def _():
            handed[m] = result
            push(handed.at[m], rows.at[m, core, OWN], HAND, m, other_section)

    def step_rows_handed(m):
        @pl.when(sec == 1)
        def _():
            step_rows(m)

    steps = [step_rows_handed, step_pass, step_last_rows, step_project, step_attend,
             step_heads, step_out, step_merge, step_finish]

    def tick(t, carry):
        for k in reversed(range(len(steps))):
            since = t - k
            run = (since >= 0) & (since <= (BATCHES - 1) * OFFSET)
            if OFFSET > 1:
                run = run & (since % OFFSET == 0)

            @pl.when(run)
            def _(k=k, since=since):
                steps[k](since // OFFSET)
        return carry
    lax.fori_loop(0, len(steps) + (BATCHES - 1) * OFFSET, tick, 0)

    def drain(m, carry):
        await_bytes(rows.at[0, 0, pl.ds(0, 4)], send.at[m, ROWS1])
        await_bytes(rows.at[0, 0, pl.ds(0, 3)], send.at[m, ROWS2])
        await_bytes(rows.at[0, 0], send.at[m, ROWS_SIB])
        await_bytes(sums.at[0, pl.ds(0, 15)], send.at[m, SUMS])
        await_bytes(sq_recv.at[0, pl.ds(0, 7)], send.at[m, SQUARES])
        await_bytes(heads.at[0, 0, pl.ds(0, 7)], send.at[m, HEADS])
        await_bytes(heads.at[0, 0], send.at[m, HEADS_SIB])
        await_bytes(out1.at[0], send.at[m, OUT1])
        await_bytes(out2.at[0], send.at[m, OUT2])

        @pl.when(sec == 0)
        def _():
            await_bytes(handed.at[0], send.at[m, HAND])
        return carry
    lax.fori_loop(0, BATCHES, drain, 0)


def body(draft_rows, norm_gain, w_query, w_keyval, w_out, kv_cache, tree_counts, cache_lengths, tree_parents):
    T, N = SLOTS, BATCHES
    feats = draft_rows.shape[1]
    width = w_query.shape[2]
    positions = kv_cache.shape[3]
    half = width // 2 + HEAD_DIM
    lanes = width // HEAD_DIM * T
    blocks = positions // KEY_BLOCK
    vmem = pl.BlockSpec(memory_space=pltpu.VMEM)
    smem = pl.BlockSpec(memory_space=pltpu.SMEM)
    anywhere = pl.BlockSpec(memory_space=pl.ANY)
    result = pl.pallas_call(
        kernel,
        out_shape=jax.ShapeDtypeStruct((2, TREE, feats), BF16),
        in_specs=[anywhere, vmem, anywhere, anywhere, anywhere, anywhere, vmem, smem, smem],
        out_specs=vmem,
        scratch_shapes=[
            pltpu.VMEM((N, 2, NZ, 2, T, feats), BF16),
            pltpu.VMEM((2, 8, feats), F32),
            pltpu.VMEM((2, feats, half), BF16),
            pltpu.VMEM((width, feats), BF16),
            pltpu.VMEM((positions, HEAD_DIM), BF16),
            pltpu.VMEM((positions, HEAD_DIM), BF16),
            pltpu.VMEM((blocks, HEAD_DIM, KEY_BLOCK), BF16),
            pltpu.VMEM((N, CHIPS, 2, T, half), BF16),
            pltpu.VMEM((N, 2 * CHIPS, T, half), BF16),
            pltpu.VMEM((N, CHIPS, 2, T, HEAD_DIM), BF16),
            pltpu.VMEM((N, CHIPS, T, HEAD_DIM), BF16),
            pltpu.VMEM((TREE, HEAD_DIM), BF16),
            pltpu.VMEM((TREE, HEAD_DIM), BF16),
            pltpu.VMEM((TREE, TREE), BF16),
            pltpu.VMEM((blocks, KEY_BLOCK, lanes), F32),
            pltpu.VMEM((N, 2, CHIPS, T, width), BF16),
            pltpu.VMEM((N, NZ, 2, T, feats), BF16),
            pltpu.VMEM((N, 3, 2, T, feats), BF16),
            pltpu.VMEM((N, 2, 2, T, feats), BF16),
            pltpu.VMEM((N, 4, 2, T, feats), BF16),
            pltpu.VMEM((N, 2, T, feats), BF16),
            pltpu.SemaphoreType.DMA((N, 10)),
            pltpu.SemaphoreType.DMA((N, 10)),
            pltpu.SemaphoreType.DMA((5,)),
            pltpu.SemaphoreType.DMA((3,)),
            pltpu.SemaphoreType.DMA((3,)),
        ],
        compiler_params=pltpu.CompilerParams(
            collective_id=0, has_side_effects=True, vmem_limit_bytes=40 << 20),
        name="two_layers",
    )(
        draft_rows.reshape(2, TREE, feats), norm_gain, w_query, w_keyval, w_out, kv_cache,
        tree_parents, tree_counts, cache_lengths,
    )
    return result.reshape(1, 2 * TREE, feats)


def solution(mesh):
    placed = (
        P("tp", "req"),
        P("section", "req"),
        P("section", "req", "tp"),
        P("section", None, "req", "tp"),
        P("section", "tp", "req"),
        P("section", "req", None, None, "tp"),
        P("req"),
        P("req"),
        P("req", None),
    )
    return jax.shard_map(
        body, mesh=mesh, in_specs=placed, out_specs=P("section", "tp", "req"), check_vma=False
    )
```

```python
import functools

import jax
import jax.numpy as jnp
from jax import lax
from jax.experimental import pallas as pl
from jax.experimental.pallas import tpu as pltpu
from jax.sharding import PartitionSpec as P

MESH = pl.DeviceIdType.MESH
F32, BF16 = jnp.float32, jnp.bfloat16

D = 8192
HEAD_DIM = 128
TREE = 64
EPSILON = 1e-05

BATCHES = 4
SLOTS = TREE // BATCHES
PLACES = (0, 3, 6, 7, 14, 21, 23, 26, 30)
OFFSET = 2
KEY_BLOCK = 1024
NX, NY, NZ = 4, 2, 8
CHIPS = NX * NY
OWN = 2
SCORE_SCALE = HEAD_DIM ** -0.5 * 1.4426950408889634
LOW = -1e30

ROWS1, ROWS2, ROWS_SIB, SUMS, SQUARES, HEADS, HEADS_SIB, OUT1, OUT2, HAND = range(10)


def dot(a, b):
    return jnp.dot(a, b, preferred_element_type=F32)


def dot_nt(a, b):
    return lax.dot_general(a, b, (((1,), (1,)), ((), ())), preferred_element_type=F32)


def kernel(
    draft, gain, w_query, w_keyval, w_out, cache, parents_in, counts, lengths, out,
    parents, rows, gains, w_in, w_o, keys, values, values_t, part, sums, sq_send, sq_recv,
    keys_new, values_new, reach, scores, heads, outp, out1, merged, out2, handed,
    send, recv, local, sib_send, sib_recv,
):
    T = SLOTS
    sec = lax.axis_index("section")
    req = lax.axis_index("req")
    z = lax.axis_index("tp")
    chip, core = req // 2, req % 2
    x, y = chip // NY, chip % NY
    key_blocks, key_block = scores.shape[0], scores.shape[1]
    lanes = scores.shape[2]

    def along(by):
        return (sec, req, (z + by + NZ) % NZ)

    sibling = (sec, chip * 2 + (1 - core), z)

    def planar(dx, dy, dc):
        to_chip = ((x + dx) % NX) * NY + (y + dy) % NY
        to_core = (core + dc) % 2
        return to_chip, to_core, (sec, to_chip * 2 + to_core, z)

    other_section = (1 - sec, req, z)
    offsets = [(dx, dy) for dx in range(NX) for dy in range(NY)]
    near = (1, -1, 2, -2)

    def push(src, dst, phase, m, device):
        pltpu.make_async_remote_copy(
            src_ref=src, dst_ref=dst, send_sem=send.at[m, phase], recv_sem=recv.at[m, phase],
            device_id=device, device_id_type=MESH,
        ).start()

    def await_bytes(ref, sem):
        pltpu.make_async_copy(ref, ref, sem).wait()

    @pl.when(sec == 0)
    def _():
        for m in range(BATCHES):
            pltpu.make_async_copy(
                draft.at[:, pl.ds(m * T, T)], rows.at[m, core, OWN], recv.at[m, HAND]
            ).start()

    half = w_in.shape[2] - HEAD_DIM
    loads = [
        pltpu.make_async_copy(
            w_query.at[0, :, pl.ds(pl.multiple_of(core * half, 128), half)],
            w_in.at[core, :, pl.ds(0, half)], local.at[0]),
        pltpu.make_async_copy(
            w_keyval.at[0, core], w_in.at[core, :, pl.ds(half, HEAD_DIM)], local.at[1]),
        pltpu.make_async_copy(cache.at[0, 0, 1], values, local.at[2]),
        pltpu.make_async_copy(cache.at[0, 0, 0], keys, local.at[3]),
        pltpu.make_async_copy(w_out.at[0], w_o, local.at[4]),
        pltpu.make_async_copy(parents_in, parents, local.at[5]),
    ]
    for load in loads:
        load.start()
    gains[core] = jnp.broadcast_to(gain[...].astype(F32), gains.shape[1:])

    barrier = pltpu.get_barrier_semaphore()
    partners = [along(by) for by in near] + [sibling, other_section]
    partners += [planar(dx, dy, dc)[2] for dx, dy in offsets if (dx, dy) != (0, 0) for dc in range(2)]
    for device in partners:
        pl.semaphore_signal(barrier, inc=1, device_id=device, device_id_type=MESH)
    pl.semaphore_wait(barrier, len(partners))

    def step_rows(m):
        await_bytes(rows.at[0, 0, 0], recv.at[m, HAND])
        for by in near:
            push(rows.at[m, core, OWN], rows.at[m, core, OWN - by], ROWS1, m, along(by))

    to_sibling = [
        pltpu.make_async_remote_copy(
            src_ref=gains.at[core], dst_ref=gains.at[core], send_sem=sib_send.at[0], recv_sem=sib_recv.at[0],
            device_id=sibling, device_id_type=MESH),
        pltpu.make_async_remote_copy(
            src_ref=w_query.at[0, :, pl.ds(pl.multiple_of((1 - core) * half, 128), half)],
            dst_ref=w_in.at[core, :, pl.ds(0, half)], send_sem=sib_send.at[1], recv_sem=sib_recv.at[1],
            device_id=sibling, device_id_type=MESH),
        pltpu.make_async_remote_copy(
            src_ref=w_keyval.at[0, 1 - core], dst_ref=w_in.at[core, :, pl.ds(half, HEAD_DIM)],
            send_sem=sib_send.at[2], recv_sem=sib_recv.at[2], device_id=sibling, device_id_type=MESH),
    ]
    for copy in to_sibling:
        copy.start()

    diagonal = lax.broadcasted_iota(jnp.int32, (HEAD_DIM, HEAD_DIM), 0) == lax.broadcasted_iota(
        jnp.int32, (HEAD_DIM, HEAD_DIM), 1)
    identity = jnp.where(diagonal, 1.0, 0.0).astype(BF16)

    def weights_ready():
        loads[0].wait()
        loads[1].wait()
        for copy in to_sibling:
            copy.wait()

    def prepare():
        loads[5].wait()
        row_index = lax.broadcasted_iota(jnp.int32, (TREE, TREE), 0)
        col_index = lax.broadcasted_iota(jnp.int32, (TREE, TREE), 1)
        closure = jnp.where((parents[...] == row_index) | (row_index == col_index), 1.0, 0.0)
        for _ in range(6):
            closure = jnp.minimum(dot(closure.astype(BF16), closure.astype(BF16)), 1.0)
        reach[...] = closure.astype(BF16)
        keys_new[...] = jnp.zeros_like(keys_new)
        values_new[...] = jnp.zeros_like(values_new)

        loads[2].wait()

        def turn(b, carry):
            values_t[b] = dot_nt(identity, values[pl.ds(pl.multiple_of(b * key_block, key_block), key_block), :]).astype(BF16)
            return carry
        lax.fori_loop(0, key_blocks, turn, 0)
        loads[3].wait()
        loads[4].wait()

    length = lengths[0]
    count = counts[0]

    def step_pass(m):
        await_bytes(rows.at[0, 0, pl.ds(0, 4)], recv.at[m, ROWS1])
        push(rows.at[m, core, 0], rows.at[m, core, 7], ROWS2, m, along(1))
        push(rows.at[m, core, 4], rows.at[m, core, 5], ROWS2, m, along(-1))
        push(rows.at[m, core, 0, 0], rows.at[m, core, 6, 0], ROWS2, m, along(2))
        push(rows.at[m, core, 4, 1], rows.at[m, core, 6, 1], ROWS2, m, along(-2))
        push(rows.at[m, core, pl.ds(0, 5)], rows.at[m, core, pl.ds(0, 5)], ROWS_SIB, m, sibling)

    def step_last_rows(m):
        await_bytes(rows.at[0, 0, pl.ds(0, 3)], recv.at[m, ROWS2])
        push(rows.at[m, core, pl.ds(5, 3)], rows.at[m, core, pl.ds(5, 3)], ROWS_SIB, m, sibling)

    def step_project(m):
        await_bytes(rows.at[0, 0], recv.at[m, ROWS_SIB])
        pl.when(m == 0)(weights_ready)
        total_sq = None
        total = None
        for s in range(2):
            block = rows[m, s].reshape(CHIPS * 2 * T, rows.shape[-1]).astype(F32)
            sq = jnp.sum(block * block, axis=1, keepdims=True)
            scaled = (block * gains[s, 0:1, :]).astype(BF16)
            product = dot(scaled, w_in[s])
            total = product if total is None else total + product
            total_sq = sq if total_sq is None else total_sq + sq
        part[m] = total.reshape(CHIPS, 2, T, total.shape[1]).astype(BF16)
        wide = jnp.broadcast_to(total_sq, (CHIPS * 2 * T, HEAD_DIM))
        lane = lax.broadcasted_iota(jnp.int32, wide.shape, 1)
        high = wide.astype(BF16)
        low = (wide - high.astype(F32)).astype(BF16)
        packed = jnp.where(lane == 0, high.astype(F32), jnp.where(lane == 1, low.astype(F32), 0.0))
        sq_send[m] = packed.reshape(CHIPS, 2, T, HEAD_DIM).astype(BF16)
        for dx, dy in offsets:
            for dc in range(2):
                if (dx, dy, dc) == (0, 0, 0):
                    continue
                to_chip, to_core, device = planar(dx, dy, dc)
                place = (to_chip - z + OWN + NZ) % NZ
                push(part.at[m, place, to_core], sums.at[m, dc * CHIPS + dx * NY + dy], SUMS, m, device)
                if dc == 0:
                    push(sq_send.at[m, place, to_core], sq_recv.at[m, dx * NY + dy], SQUARES, m, device)

    def step_attend(m):
        pl.when(m == 0)(prepare)
        await_bytes(sums.at[0, pl.ds(0, 15)], recv.at[m, SUMS])
        await_bytes(sq_recv.at[0, pl.ds(0, 7)], recv.at[m, SQUARES])
        place = (chip - z + OWN + NZ) % NZ
        same = part[m, place, core].astype(F32)
        squares = sq_send[m, place, core].astype(F32)
        for k in range(1, CHIPS):
            same = same + sums[m, k].astype(F32)
            squares = squares + sq_recv[m, k].astype(F32)
        other = sums[m, CHIPS].astype(F32)
        for k in range(CHIPS + 1, 2 * CHIPS):
            other = other + sums[m, k].astype(F32)
        inverse = lax.rsqrt(jnp.sum(squares, axis=1, keepdims=True) / D + EPSILON)
        same = same * inverse
        other = other * inverse
        first = jnp.where(core == 0, same, other).astype(BF16)
        second = jnp.where(core == 0, other, same).astype(BF16)
        query = jnp.concatenate(
            [g[:, h * HEAD_DIM:(h + 1) * HEAD_DIM] for g in (first, second) for h in range(half // HEAD_DIM)], axis=0)
        slots = pl.ds(pl.multiple_of(m * T, T), T)
        keys_new[slots, :] = first[:, half:]
        values_new[slots, :] = second[:, half:]

        lane_slot = lax.broadcasted_iota(jnp.int32, (TREE, lanes), 1) % T + m * T
        pick = jnp.where(lax.broadcasted_iota(jnp.int32, (TREE, lanes), 0) == lane_slot, 1.0, 0.0).astype(BF16)
        reached = dot(reach[...], pick) > 0.5
        tree_scores = jnp.where(reached, dot_nt(keys_new[...], query), LOW)
        top = jnp.max(tree_scores, axis=0, keepdims=True)
        position = lax.broadcasted_iota(jnp.int32, (key_block, lanes), 0)
        for b in range(key_blocks):
            block = dot_nt(keys[b * key_block:(b + 1) * key_block, :], query)
            block = jnp.where(position < length - b * key_block, block, LOW)
            scores[b] = block
            top = jnp.maximum(top, jnp.max(block, axis=0, keepdims=True))
        weights = jnp.exp2((tree_scores - top) * SCORE_SCALE)
        total = jnp.sum(weights, axis=0, keepdims=True)
        values_new_t = dot_nt(identity, values_new[...]).astype(BF16)
        mixed = dot(values_new_t, weights.astype(BF16))
        for b in range(key_blocks):
            weights = jnp.exp2((scores[b] - top) * SCORE_SCALE)
            total = total + jnp.sum(weights, axis=0, keepdims=True)
            mixed = mixed + dot(values_t[b], weights.astype(BF16))
        live = lax.broadcasted_iota(jnp.int32, (1, lanes), 1) % T + m * T < count
        mixed = jnp.where(live, mixed / total, 0.0).T.astype(BF16)
        for h in range(lanes // T):
            heads[m, core, chip, :, h * HEAD_DIM:(h + 1) * HEAD_DIM] = mixed[h * T:(h + 1) * T, :]
        for dx, dy in offsets:
            if (dx, dy) != (0, 0):
                push(heads.at[m, core, chip], heads.at[m, core, chip], HEADS, m, planar(dx, dy, 0)[2])

    def step_heads(m):
        await_bytes(heads.at[0, 0, pl.ds(0, 7)], recv.at[m, HEADS])
        push(heads.at[m, core], heads.at[m, core], HEADS_SIB, m, sibling)

    def step_out(m):
        await_bytes(heads.at[0, 0], recv.at[m, HEADS_SIB])
        product = dot(heads[m].reshape(2 * CHIPS * T, heads.shape[-1]), w_o[...]).astype(BF16)
        product = product.reshape(2, CHIPS, T, product.shape[1])
        for i in range(2):
            outp[m, :, i] = product[i]
        push(outp.at[m, (z + 3) % NZ], out1.at[m, 0], OUT1, m, along(1))
        push(outp.at[m, (z + 5) % NZ], out1.at[m, 1], OUT1, m, along(-1))
        push(outp.at[m, (z + 4) % NZ, 0], out1.at[m, 2, 0], OUT1, m, along(2))
        push(outp.at[m, (z + 4) % NZ, 1], out1.at[m, 2, 1], OUT1, m, along(-2))
        push(outp.at[m, (z + 1) % NZ], out2.at[m, 2], OUT2, m, along(1))
        push(outp.at[m, (z + 7) % NZ], out2.at[m, 3], OUT2, m, along(-1))

    def step_merge(m):
        await_bytes(out1.at[0], recv.at[m, OUT1])
        for side, by in enumerate((2, -2)):
            both = outp[m, (z + by + NZ) % NZ].astype(F32) + out1[m, side].astype(F32)
            merged[m, side] = both.astype(BF16)
            merged[m, side, side] = (both[side] + out1[m, 2, side].astype(F32)).astype(BF16)
            push(merged.at[m, side], out2.at[m, side], OUT2, m, along(by))

    def step_finish(m):
        await_bytes(out2.at[0], recv.at[m, OUT2])
        total = outp[m, z].astype(F32)
        for k in range(4):
            total = total + out2[m, k].astype(F32)
        result = (total + rows[m, core, OWN].astype(F32)).astype(BF16)
        out[:, pl.ds(pl.multiple_of(m * T, T), T), :] = result

        @pl.when(sec == 0)
        def _():
            handed[m] = result
            push(handed.at[m], rows.at[m, core, OWN], HAND, m, other_section)

    steps = [step_rows, step_pass, step_last_rows, step_project, step_attend,
             step_heads, step_out, step_merge, step_finish]

    def tick(t, carry):
        for k in reversed(range(len(steps))):
            since = t - PLACES[k]
            run = (since >= 0) & (since <= (BATCHES - 1) * OFFSET)
            if OFFSET > 1:
                run = run & (since % OFFSET == 0)

            @pl.when(run)
            def _(k=k, since=since):
                steps[k](since // OFFSET)
        return carry
    lax.fori_loop(0, PLACES[-1] + (BATCHES - 1) * OFFSET + 1, tick, 0)

    def drain(m, carry):
        await_bytes(rows.at[0, 0, pl.ds(0, 4)], send.at[m, ROWS1])
        await_bytes(rows.at[0, 0, pl.ds(0, 3)], send.at[m, ROWS2])
        await_bytes(rows.at[0, 0], send.at[m, ROWS_SIB])
        await_bytes(sums.at[0, pl.ds(0, 15)], send.at[m, SUMS])
        await_bytes(sq_recv.at[0, pl.ds(0, 7)], send.at[m, SQUARES])
        await_bytes(heads.at[0, 0, pl.ds(0, 7)], send.at[m, HEADS])
        await_bytes(heads.at[0, 0], send.at[m, HEADS_SIB])
        await_bytes(out1.at[0], send.at[m, OUT1])
        await_bytes(out2.at[0], send.at[m, OUT2])

        @pl.when(sec == 0)
        def _():
            await_bytes(handed.at[0], send.at[m, HAND])
        return carry
    lax.fori_loop(0, BATCHES, drain, 0)


def body(draft_rows, norm_gain, w_query, w_keyval, w_out, kv_cache, tree_counts, cache_lengths, tree_parents):
    T, N = SLOTS, BATCHES
    feats = draft_rows.shape[1]
    width = w_query.shape[2]
    positions = kv_cache.shape[3]
    half = width // 2 + HEAD_DIM
    lanes = width // HEAD_DIM * T
    blocks = positions // KEY_BLOCK
    vmem = pl.BlockSpec(memory_space=pltpu.VMEM)
    smem = pl.BlockSpec(memory_space=pltpu.SMEM)
    anywhere = pl.BlockSpec(memory_space=pltpu.HBM)
    result = pl.pallas_call(
        kernel,
        out_shape=jax.ShapeDtypeStruct((2, TREE, feats), BF16),
        in_specs=[anywhere, vmem, anywhere, anywhere, anywhere, anywhere, anywhere, smem, smem],
        out_specs=vmem,
        scratch_shapes=[
            pltpu.VMEM((1, TREE), jnp.int32),
            pltpu.VMEM((N, 2, NZ, 2, T, feats), BF16),
            pltpu.VMEM((2, 8, feats), F32),
            pltpu.VMEM((2, feats, half), BF16),
            pltpu.VMEM((width, feats), BF16),
            pltpu.VMEM((positions, HEAD_DIM), BF16),
            pltpu.VMEM((positions, HEAD_DIM), BF16),
            pltpu.VMEM((blocks, HEAD_DIM, KEY_BLOCK), BF16),
            pltpu.VMEM((N, CHIPS, 2, T, half), BF16),
            pltpu.VMEM((N, 2 * CHIPS, T, half), BF16),
            pltpu.VMEM((N, CHIPS, 2, T, HEAD_DIM), BF16),
            pltpu.VMEM((N, CHIPS, T, HEAD_DIM), BF16),
            pltpu.VMEM((TREE, HEAD_DIM), BF16),
            pltpu.VMEM((TREE, HEAD_DIM), BF16),
            pltpu.VMEM((TREE, TREE), BF16),
            pltpu.VMEM((blocks, KEY_BLOCK, lanes), F32),
            pltpu.VMEM((N, 2, CHIPS, T, width), BF16),
            pltpu.VMEM((N, NZ, 2, T, feats), BF16),
            pltpu.VMEM((N, 3, 2, T, feats), BF16),
            pltpu.VMEM((N, 2, 2, T, feats), BF16),
            pltpu.VMEM((N, 4, 2, T, feats), BF16),
            pltpu.VMEM((N, 2, T, feats), BF16),
            pltpu.SemaphoreType.DMA((N, 10)),
            pltpu.SemaphoreType.DMA((N, 10)),
            pltpu.SemaphoreType.DMA((6,)),
            pltpu.SemaphoreType.DMA((3,)),
            pltpu.SemaphoreType.DMA((3,)),
        ],
        compiler_params=pltpu.CompilerParams(
            collective_id=0, has_side_effects=True, vmem_limit_bytes=58 << 20),
        name="two_layers",
    )(
        draft_rows.reshape(2, TREE, feats), norm_gain, w_query, w_keyval, w_out, kv_cache,
        tree_parents, tree_counts, cache_lengths,
    )
    return result.reshape(1, 2 * TREE, feats)


def solution(mesh):
    placed = (
        P("tp", "req"),
        P("section", "req"),
        P("section", "req", "tp"),
        P("section", None, "req", "tp"),
        P("section", "tp", "req"),
        P("section", "req", None, None, "tp"),
        P("req"),
        P("req"),
        P("req", None),
    )
    return jax.shard_map(
        body, mesh=mesh, in_specs=placed, out_specs=P("section", "tp", "req"), check_vma=False
    )
```

```python
import functools

import jax
import jax.numpy as jnp
from jax import lax
from jax.experimental import pallas as pl
from jax.experimental.pallas import tpu as pltpu
from jax.sharding import PartitionSpec as P

MESH = pl.DeviceIdType.MESH
F32, BF16 = jnp.float32, jnp.bfloat16

D = 8192
HEAD_DIM = 128
TREE = 64
EPSILON = 1e-05

BATCHES = 4
SLOTS = TREE // BATCHES
PLACES = (0, 3, 6, 7, 13, 19, 21, 24, 28)
OFFSET = 2
KEY_BLOCK = 1024
NX, NY, NZ = 4, 2, 8
CHIPS = NX * NY
OWN = 2
SCORE_SCALE = HEAD_DIM ** -0.5 * 1.4426950408889634
LOW = -1e30

ROWS1, ROWS2, ROWS_SIB, SUMS, SQUARES, HEADS, HEADS_SIB, OUT1, OUT2, HAND = range(10)


def dot(a, b):
    return jnp.dot(a, b, preferred_element_type=F32)


def dot_nt(a, b):
    return lax.dot_general(a, b, (((1,), (1,)), ((), ())), preferred_element_type=F32)


def kernel(
    draft, gain, w_query, w_keyval, w_out, cache, parents_in, counts, lengths, out,
    parents, rows, gains, w_in, w_o, keys, values, values_t, part, sums, sq_send, sq_recv,
    keys_new, values_new, reach, scores, heads, outp, out1, merged, out2, handed,
    send, recv, local, sib_send, sib_recv, out_sem,
):
    T = SLOTS
    sec = lax.axis_index("section")
    req = lax.axis_index("req")
    z = lax.axis_index("tp")
    chip, core = req // 2, req % 2
    x, y = chip // NY, chip % NY
    key_blocks, key_block = scores.shape[0], scores.shape[1]
    lanes = scores.shape[2]

    def along(by):
        return (sec, req, (z + by + NZ) % NZ)

    sibling = (sec, chip * 2 + (1 - core), z)

    def planar(dx, dy, dc):
        to_chip = ((x + dx) % NX) * NY + (y + dy) % NY
        to_core = (core + dc) % 2
        return to_chip, to_core, (sec, to_chip * 2 + to_core, z)

    other_section = (1 - sec, req, z)
    offsets = [(2, 1), (2, 0), (1, 1), (3, 1), (1, 0), (3, 0), (0, 1), (0, 0)]
    near = (1, -1, 2, -2)

    def push(src, dst, phase, m, device):
        pltpu.make_async_remote_copy(
            src_ref=src, dst_ref=dst, send_sem=send.at[m, phase], recv_sem=recv.at[m, phase],
            device_id=device, device_id_type=MESH,
        ).start()

    def await_bytes(ref, sem):
        pltpu.make_async_copy(ref, ref, sem).wait()

    @pl.when(sec == 0)
    def _():
        for m in range(BATCHES):
            pltpu.make_async_copy(
                draft.at[:, pl.ds(m * T, T)], rows.at[m, core, OWN], recv.at[m, HAND]
            ).start()

    half = w_in.shape[2] - HEAD_DIM
    loads = [
        pltpu.make_async_copy(
            w_query.at[0, :, pl.ds(pl.multiple_of(core * half, 128), half)],
            w_in.at[core, :, pl.ds(0, half)], local.at[0]),
        pltpu.make_async_copy(
            w_keyval.at[0, core], w_in.at[core, :, pl.ds(half, HEAD_DIM)], local.at[1]),
        pltpu.make_async_copy(cache.at[0, 0, 1], values, local.at[2]),
        pltpu.make_async_copy(cache.at[0, 0, 0], keys, local.at[3]),
        pltpu.make_async_copy(w_out.at[0], w_o, local.at[4]),
        pltpu.make_async_copy(parents_in, parents, local.at[5]),
    ]
    for load in loads:
        load.start()
    gains[core] = jnp.broadcast_to(gain[...].astype(F32), gains.shape[1:])

    barrier = pltpu.get_barrier_semaphore()
    partners = [along(by) for by in near] + [sibling, other_section]
    partners += [planar(dx, dy, dc)[2] for dx, dy in offsets if (dx, dy) != (0, 0) for dc in range(2)]
    for device in partners:
        pl.semaphore_signal(barrier, inc=1, device_id=device, device_id_type=MESH)
    pl.semaphore_wait(barrier, len(partners))

    def step_rows(m):
        await_bytes(rows.at[0, 0, 0], recv.at[m, HAND])
        for by in near:
            push(rows.at[m, core, OWN], rows.at[m, core, OWN - by], ROWS1, m, along(by))

    to_sibling = [
        pltpu.make_async_remote_copy(
            src_ref=gains.at[core], dst_ref=gains.at[core], send_sem=sib_send.at[0], recv_sem=sib_recv.at[0],
            device_id=sibling, device_id_type=MESH),
        pltpu.make_async_remote_copy(
            src_ref=w_query.at[0, :, pl.ds(pl.multiple_of((1 - core) * half, 128), half)],
            dst_ref=w_in.at[core, :, pl.ds(0, half)], send_sem=sib_send.at[1], recv_sem=sib_recv.at[1],
            device_id=sibling, device_id_type=MESH),
        pltpu.make_async_remote_copy(
            src_ref=w_keyval.at[0, 1 - core], dst_ref=w_in.at[core, :, pl.ds(half, HEAD_DIM)],
            send_sem=sib_send.at[2], recv_sem=sib_recv.at[2], device_id=sibling, device_id_type=MESH),
    ]
    for copy in to_sibling:
        copy.start()

    diagonal = lax.broadcasted_iota(jnp.int32, (HEAD_DIM, HEAD_DIM), 0) == lax.broadcasted_iota(
        jnp.int32, (HEAD_DIM, HEAD_DIM), 1)
    identity = jnp.where(diagonal, 1.0, 0.0).astype(BF16)

    def weights_ready():
        loads[0].wait()
        loads[1].wait()
        for copy in to_sibling:
            copy.wait()

    def prepare():
        loads[5].wait()
        row_index = lax.broadcasted_iota(jnp.int32, (TREE, TREE), 0)
        col_index = lax.broadcasted_iota(jnp.int32, (TREE, TREE), 1)
        closure = jnp.where((parents[...] == row_index) | (row_index == col_index), 1.0, 0.0)
        for _ in range(6):
            closure = jnp.minimum(dot(closure.astype(BF16), closure.astype(BF16)), 1.0)
        reach[...] = closure.astype(BF16)
        keys_new[...] = jnp.zeros_like(keys_new)
        values_new[...] = jnp.zeros_like(values_new)

        loads[2].wait()

        def turn(b, carry):
            values_t[b] = dot_nt(identity, values[pl.ds(pl.multiple_of(b * key_block, key_block), key_block), :]).astype(BF16)
            return carry
        lax.fori_loop(0, key_blocks, turn, 0)
        loads[3].wait()
        loads[4].wait()

    length = lengths[0]
    count = counts[0]

    def step_pass(m):
        await_bytes(rows.at[0, 0, pl.ds(0, 4)], recv.at[m, ROWS1])
        push(rows.at[m, core, 0], rows.at[m, core, 7], ROWS2, m, along(1))
        push(rows.at[m, core, 4], rows.at[m, core, 5], ROWS2, m, along(-1))
        push(rows.at[m, core, 0, 0], rows.at[m, core, 6, 0], ROWS2, m, along(2))
        push(rows.at[m, core, 4, 1], rows.at[m, core, 6, 1], ROWS2, m, along(-2))
        push(rows.at[m, core, pl.ds(0, 5)], rows.at[m, core, pl.ds(0, 5)], ROWS_SIB, m, sibling)

    def step_last_rows(m):
        await_bytes(rows.at[0, 0, pl.ds(0, 3)], recv.at[m, ROWS2])
        push(rows.at[m, core, pl.ds(5, 3)], rows.at[m, core, pl.ds(5, 3)], ROWS_SIB, m, sibling)

    def step_project(m):
        await_bytes(rows.at[0, 0], recv.at[m, ROWS_SIB])
        pl.when(m == 0)(weights_ready)
        total_sq = None
        total = None
        for s in range(2):
            block = rows[m, s].reshape(CHIPS * 2 * T, rows.shape[-1]).astype(F32)
            sq = jnp.sum(block * block, axis=1, keepdims=True)
            scaled = (block * gains[s, 0:1, :]).astype(BF16)
            product = dot(scaled, w_in[s])
            total = product if total is None else total + product
            total_sq = sq if total_sq is None else total_sq + sq
        part[m] = total.reshape(CHIPS, 2, T, total.shape[1]).astype(BF16)
        wide = jnp.broadcast_to(total_sq, (CHIPS * 2 * T, HEAD_DIM))
        lane = lax.broadcasted_iota(jnp.int32, wide.shape, 1)
        high = wide.astype(BF16)
        low = (wide - high.astype(F32)).astype(BF16)
        packed = jnp.where(lane == 0, high.astype(F32), jnp.where(lane == 1, low.astype(F32), 0.0))
        sq_send[m] = packed.reshape(CHIPS, 2, T, HEAD_DIM).astype(BF16)
        for dx, dy in offsets:
            for dc in range(2):
                if (dx, dy, dc) == (0, 0, 0):
                    continue
                to_chip, to_core, device = planar(dx, dy, dc)
                place = (to_chip - z + OWN + NZ) % NZ
                push(part.at[m, place, to_core], sums.at[m, dc * CHIPS + dx * NY + dy], SUMS, m, device)
                if dc == 0:
                    push(sq_send.at[m, place, to_core], sq_recv.at[m, dx * NY + dy], SQUARES, m, device)

    def step_attend(m):
        pl.when(m == 0)(prepare)
        await_bytes(sums.at[0, pl.ds(0, 15)], recv.at[m, SUMS])
        await_bytes(sq_recv.at[0, pl.ds(0, 7)], recv.at[m, SQUARES])
        place = (chip - z + OWN + NZ) % NZ
        same = part[m, place, core].astype(F32)
        squares = sq_send[m, place, core].astype(F32)
        for k in range(1, CHIPS):
            same = same + sums[m, k].astype(F32)
            squares = squares + sq_recv[m, k].astype(F32)
        other = sums[m, CHIPS].astype(F32)
        for k in range(CHIPS + 1, 2 * CHIPS):
            other = other + sums[m, k].astype(F32)
        inverse = lax.rsqrt(jnp.sum(squares, axis=1, keepdims=True) / D + EPSILON)
        same = same * inverse
        other = other * inverse
        first = jnp.where(core == 0, same, other).astype(BF16)
        second = jnp.where(core == 0, other, same).astype(BF16)
        query = jnp.concatenate(
            [g[:, h * HEAD_DIM:(h + 1) * HEAD_DIM] for g in (first, second) for h in range(half // HEAD_DIM)], axis=0)
        slots = pl.ds(pl.multiple_of(m * T, T), T)
        keys_new[slots, :] = first[:, half:]
        values_new[slots, :] = second[:, half:]

        lane_slot = lax.broadcasted_iota(jnp.int32, (TREE, lanes), 1) % T + m * T
        pick = jnp.where(lax.broadcasted_iota(jnp.int32, (TREE, lanes), 0) == lane_slot, 1.0, 0.0).astype(BF16)
        reached = dot(reach[...], pick) > 0.5
        tree_scores = jnp.where(reached, dot_nt(keys_new[...], query), LOW)
        top = jnp.max(tree_scores, axis=0, keepdims=True)
        position = lax.broadcasted_iota(jnp.int32, (key_block, lanes), 0)
        for b in range(key_blocks):
            block = dot_nt(keys[b * key_block:(b + 1) * key_block, :], query)
            block = jnp.where(position < length - b * key_block, block, LOW)
            scores[b] = block
            top = jnp.maximum(top, jnp.max(block, axis=0, keepdims=True))
        weights = jnp.exp2((tree_scores - top) * SCORE_SCALE)
        total = jnp.sum(weights, axis=0, keepdims=True)
        values_new_t = dot_nt(identity, values_new[...]).astype(BF16)
        mixed = dot(values_new_t, weights.astype(BF16))
        for b in range(key_blocks):
            weights = jnp.exp2((scores[b] - top) * SCORE_SCALE)
            total = total + jnp.sum(weights, axis=0, keepdims=True)
            mixed = mixed + dot(values_t[b], weights.astype(BF16))
        live = lax.broadcasted_iota(jnp.int32, (1, lanes), 1) % T + m * T < count
        mixed = jnp.where(live, mixed / total, 0.0).T.astype(BF16)
        for h in range(lanes // T):
            heads[m, core, chip, :, h * HEAD_DIM:(h + 1) * HEAD_DIM] = mixed[h * T:(h + 1) * T, :]
        for dx, dy in offsets:
            if (dx, dy) != (0, 0):
                push(heads.at[m, core, chip], heads.at[m, core, chip], HEADS, m, planar(dx, dy, 0)[2])

    def step_heads(m):
        await_bytes(heads.at[0, 0, pl.ds(0, 7)], recv.at[m, HEADS])
        push(heads.at[m, core], heads.at[m, core], HEADS_SIB, m, sibling)

    def step_out(m):
        await_bytes(heads.at[0, 0], recv.at[m, HEADS_SIB])
        product = dot(heads[m].reshape(2 * CHIPS * T, heads.shape[-1]), w_o[...]).astype(BF16)
        product = product.reshape(2, CHIPS, T, product.shape[1])
        for i in range(2):
            outp[m, :, i] = product[i]
        push(outp.at[m, (z + 4) % NZ, 0], out1.at[m, 2, 0], OUT1, m, along(2))
        push(outp.at[m, (z + 4) % NZ, 1], out1.at[m, 2, 1], OUT1, m, along(-2))
        push(outp.at[m, (z + 3) % NZ], out1.at[m, 0], OUT1, m, along(1))
        push(outp.at[m, (z + 5) % NZ], out1.at[m, 1], OUT1, m, along(-1))
        push(outp.at[m, (z + 1) % NZ], out2.at[m, 2], OUT2, m, along(1))
        push(outp.at[m, (z + 7) % NZ], out2.at[m, 3], OUT2, m, along(-1))

    def step_merge(m):
        await_bytes(out1.at[0], recv.at[m, OUT1])
        for side, by in enumerate((2, -2)):
            both = outp[m, (z + by + NZ) % NZ].astype(F32) + out1[m, side].astype(F32)
            merged[m, side] = both.astype(BF16)
            merged[m, side, side] = (both[side] + out1[m, 2, side].astype(F32)).astype(BF16)
            push(merged.at[m, side], out2.at[m, side], OUT2, m, along(by))

    def step_finish(m):
        await_bytes(out2.at[0], recv.at[m, OUT2])
        total = outp[m, z].astype(F32)
        for k in range(4):
            total = total + out2[m, k].astype(F32)
        result = (total + rows[m, core, OWN].astype(F32)).astype(BF16)
        handed[m] = result

        @pl.when(sec == 0)
        def _():
            push(handed.at[m], rows.at[m, core, OWN], HAND, m, other_section)
        write(m).start()

    def write(m):
        return pltpu.make_async_copy(
            handed.at[m], out.at[:, pl.ds(pl.multiple_of(m * T, T), T)], out_sem.at[m])

    steps = [step_rows, step_pass, step_last_rows, step_project, step_attend,
             step_heads, step_out, step_merge, step_finish]

    def tick(t, carry):
        for k in reversed(range(len(steps))):
            since = t - PLACES[k]
            run = (since >= 0) & (since <= (BATCHES - 1) * OFFSET)
            if OFFSET > 1:
                run = run & (since % OFFSET == 0)

            @pl.when(run)
            def _(k=k, since=since):
                steps[k](since // OFFSET)
        return carry
    lax.fori_loop(0, PLACES[-1] + (BATCHES - 1) * OFFSET + 1, tick, 0)

    def drain(m, carry):
        write(m).wait()
        await_bytes(rows.at[0, 0, pl.ds(0, 4)], send.at[m, ROWS1])
        await_bytes(rows.at[0, 0, pl.ds(0, 3)], send.at[m, ROWS2])
        await_bytes(rows.at[0, 0], send.at[m, ROWS_SIB])
        await_bytes(sums.at[0, pl.ds(0, 15)], send.at[m, SUMS])
        await_bytes(sq_recv.at[0, pl.ds(0, 7)], send.at[m, SQUARES])
        await_bytes(heads.at[0, 0, pl.ds(0, 7)], send.at[m, HEADS])
        await_bytes(heads.at[0, 0], send.at[m, HEADS_SIB])
        await_bytes(out1.at[0], send.at[m, OUT1])
        await_bytes(out2.at[0], send.at[m, OUT2])

        @pl.when(sec == 0)
        def _():
            await_bytes(handed.at[0], send.at[m, HAND])
        return carry
    lax.fori_loop(0, BATCHES, drain, 0)


def body(draft_rows, norm_gain, w_query, w_keyval, w_out, kv_cache, tree_counts, cache_lengths, tree_parents):
    T, N = SLOTS, BATCHES
    feats = draft_rows.shape[1]
    width = w_query.shape[2]
    positions = kv_cache.shape[3]
    half = width // 2 + HEAD_DIM
    lanes = width // HEAD_DIM * T
    blocks = positions // KEY_BLOCK
    vmem = pl.BlockSpec(memory_space=pltpu.VMEM)
    smem = pl.BlockSpec(memory_space=pltpu.SMEM)
    anywhere = pl.BlockSpec(memory_space=pltpu.HBM)
    result = pl.pallas_call(
        kernel,
        out_shape=jax.ShapeDtypeStruct((2, TREE, feats), BF16),
        in_specs=[anywhere, vmem, anywhere, anywhere, anywhere, anywhere, anywhere, smem, smem],
        out_specs=anywhere,
        scratch_shapes=[
            pltpu.VMEM((1, TREE), jnp.int32),
            pltpu.VMEM((N, 2, NZ, 2, T, feats), BF16),
            pltpu.VMEM((2, 8, feats), F32),
            pltpu.VMEM((2, feats, half), BF16),
            pltpu.VMEM((width, feats), BF16),
            pltpu.VMEM((positions, HEAD_DIM), BF16),
            pltpu.VMEM((positions, HEAD_DIM), BF16),
            pltpu.VMEM((blocks, HEAD_DIM, KEY_BLOCK), BF16),
            pltpu.VMEM((N, CHIPS, 2, T, half), BF16),
            pltpu.VMEM((N, 2 * CHIPS, T, half), BF16),
            pltpu.VMEM((N, CHIPS, 2, T, HEAD_DIM), BF16),
            pltpu.VMEM((N, CHIPS, T, HEAD_DIM), BF16),
            pltpu.VMEM((TREE, HEAD_DIM), BF16),
            pltpu.VMEM((TREE, HEAD_DIM), BF16),
            pltpu.VMEM((TREE, TREE), BF16),
            pltpu.VMEM((blocks, KEY_BLOCK, lanes), F32),
            pltpu.VMEM((N, 2, CHIPS, T, width), BF16),
            pltpu.VMEM((N, NZ, 2, T, feats), BF16),
            pltpu.VMEM((N, 3, 2, T, feats), BF16),
            pltpu.VMEM((N, 2, 2, T, feats), BF16),
            pltpu.VMEM((N, 4, 2, T, feats), BF16),
            pltpu.VMEM((N, 2, T, feats), BF16),
            pltpu.SemaphoreType.DMA((N, 10)),
            pltpu.SemaphoreType.DMA((N, 10)),
            pltpu.SemaphoreType.DMA((6,)),
            pltpu.SemaphoreType.DMA((3,)),
            pltpu.SemaphoreType.DMA((3,)),
            pltpu.SemaphoreType.DMA((N,)),
        ],
        compiler_params=pltpu.CompilerParams(
            collective_id=0, has_side_effects=True, vmem_limit_bytes=58 << 20),
        name="two_layers",
    )(
        draft_rows.reshape(2, TREE, feats), norm_gain, w_query, w_keyval, w_out, kv_cache,
        tree_parents, tree_counts, cache_lengths,
    )
    return result.reshape(1, 2 * TREE, feats)


def solution(mesh):
    placed = (
        P("tp", "req"),
        P("section", "req"),
        P("section", "req", "tp"),
        P("section", None, "req", "tp"),
        P("section", "tp", "req"),
        P("section", "req", None, None, "tp"),
        P("req"),
        P("req"),
        P("req", None),
    )
    return jax.shard_map(
        body, mesh=mesh, in_specs=placed, out_specs=P("section", "tp", "req"), check_vma=False
    )
```

```python
import functools

import jax
import jax.numpy as jnp
from jax import lax
from jax.experimental import pallas as pl
from jax.experimental.pallas import tpu as pltpu
from jax.sharding import PartitionSpec as P

MESH = pl.DeviceIdType.MESH
F32, BF16 = jnp.float32, jnp.bfloat16

D = 8192
HEAD_DIM = 128
TREE = 64
EPSILON = 1e-05

BATCHES = 4
SLOTS = TREE // BATCHES
PLACES = (0, 3, 6, 7, 13, 19, 20, 23, 27)
OFFSET = 2
KEY_BLOCK = 1024
NX, NY, NZ = 4, 2, 8
CHIPS = NX * NY
OWN = 2
SCORE_SCALE = HEAD_DIM ** -0.5 * 1.4426950408889634
LOW = -1e30

ROWS1, ROWS2, ROWS_SIB, SUMS, SQUARES, HEADS, HEADS_SIB, OUT1, OUT2, HAND = range(10)


def dot(a, b):
    return jnp.dot(a, b, preferred_element_type=F32)


def dot_nt(a, b):
    return lax.dot_general(a, b, (((1,), (1,)), ((), ())), preferred_element_type=F32)


def kernel(
    draft, gain, w_query, w_keyval, w_out, cache, parents_in, counts, lengths, out,
    parents, rows, gains, w_in, w_o, keys, values, values_t, half_sum, half_sq, part, sums, sq_send, sq_recv,
    keys_new, values_new, reach, scores, heads, outp, out1, merged, out2, handed,
    send, recv, local, sib_send, sib_recv, out_sem,
):
    T = SLOTS
    sec = lax.axis_index("section")
    req = lax.axis_index("req")
    z = lax.axis_index("tp")
    chip, core = req // 2, req % 2
    x, y = chip // NY, chip % NY
    key_blocks, key_block = scores.shape[0], scores.shape[1]
    lanes = scores.shape[2]

    def along(by):
        return (sec, req, (z + by + NZ) % NZ)

    sibling = (sec, chip * 2 + (1 - core), z)

    def planar(dx, dy, dc):
        to_chip = ((x + dx) % NX) * NY + (y + dy) % NY
        to_core = (core + dc) % 2
        return to_chip, to_core, (sec, to_chip * 2 + to_core, z)

    other_section = (1 - sec, req, z)
    offsets = [(2, 1), (2, 0), (1, 1), (3, 1), (1, 0), (3, 0), (0, 1), (0, 0)]
    near = (1, -1, 2, -2)

    def push(src, dst, phase, m, device):
        pltpu.make_async_remote_copy(
            src_ref=src, dst_ref=dst, send_sem=send.at[m, phase], recv_sem=recv.at[m, phase],
            device_id=device, device_id_type=MESH,
        ).start()

    def await_bytes(ref, sem):
        pltpu.make_async_copy(ref, ref, sem).wait()

    @pl.when(sec == 0)
    def _():
        for m in range(BATCHES):
            pltpu.make_async_copy(
                draft.at[:, pl.ds(m * T, T)], rows.at[m, core, OWN], recv.at[m, HAND]
            ).start()

    half = w_in.shape[2] - HEAD_DIM
    loads = [
        pltpu.make_async_copy(
            w_query.at[0, :, pl.ds(pl.multiple_of(core * half, 128), half)],
            w_in.at[core, :, pl.ds(0, half)], local.at[0]),
        pltpu.make_async_copy(
            w_keyval.at[0, core], w_in.at[core, :, pl.ds(half, HEAD_DIM)], local.at[1]),
        pltpu.make_async_copy(cache.at[0, 0, 1], values, local.at[2]),
        pltpu.make_async_copy(cache.at[0, 0, 0], keys, local.at[3]),
        pltpu.make_async_copy(w_out.at[0], w_o, local.at[4]),
        pltpu.make_async_copy(parents_in, parents, local.at[5]),
    ]
    for load in loads:
        load.start()
    gains[core] = jnp.broadcast_to(gain[...].astype(F32), gains.shape[1:])

    barrier = pltpu.get_barrier_semaphore()
    partners = [along(by) for by in near] + [sibling, other_section]
    partners += [planar(dx, dy, dc)[2] for dx, dy in offsets if (dx, dy) != (0, 0) for dc in range(2)]
    for device in partners:
        pl.semaphore_signal(barrier, inc=1, device_id=device, device_id_type=MESH)
    pl.semaphore_wait(barrier, len(partners))

    def step_rows(m):
        await_bytes(rows.at[0, 0, 0], recv.at[m, HAND])
        for by in near:
            push(rows.at[m, core, OWN], rows.at[m, core, OWN - by], ROWS1, m, along(by))

    to_sibling = [
        pltpu.make_async_remote_copy(
            src_ref=gains.at[core], dst_ref=gains.at[core], send_sem=sib_send.at[0], recv_sem=sib_recv.at[0],
            device_id=sibling, device_id_type=MESH),
        pltpu.make_async_remote_copy(
            src_ref=w_query.at[0, :, pl.ds(pl.multiple_of((1 - core) * half, 128), half)],
            dst_ref=w_in.at[core, :, pl.ds(0, half)], send_sem=sib_send.at[1], recv_sem=sib_recv.at[1],
            device_id=sibling, device_id_type=MESH),
        pltpu.make_async_remote_copy(
            src_ref=w_keyval.at[0, 1 - core], dst_ref=w_in.at[core, :, pl.ds(half, HEAD_DIM)],
            send_sem=sib_send.at[2], recv_sem=sib_recv.at[2], device_id=sibling, device_id_type=MESH),
    ]
    for copy in to_sibling:
        copy.start()

    diagonal = lax.broadcasted_iota(jnp.int32, (HEAD_DIM, HEAD_DIM), 0) == lax.broadcasted_iota(
        jnp.int32, (HEAD_DIM, HEAD_DIM), 1)
    identity = jnp.where(diagonal, 1.0, 0.0).astype(BF16)

    def weights_ready():
        loads[0].wait()
        loads[1].wait()
        for copy in to_sibling:
            copy.wait()

    def prepare():
        loads[5].wait()
        row_index = lax.broadcasted_iota(jnp.int32, (TREE, TREE), 0)
        col_index = lax.broadcasted_iota(jnp.int32, (TREE, TREE), 1)
        closure = jnp.where((parents[...] == row_index) | (row_index == col_index), 1.0, 0.0)
        for _ in range(6):
            closure = jnp.minimum(dot(closure.astype(BF16), closure.astype(BF16)), 1.0)
        reach[...] = closure.astype(BF16)
        keys_new[...] = jnp.zeros_like(keys_new)
        values_new[...] = jnp.zeros_like(values_new)

        loads[2].wait()

        def turn(b, carry):
            values_t[b] = dot_nt(identity, values[pl.ds(pl.multiple_of(b * key_block, key_block), key_block), :]).astype(BF16)
            return carry
        lax.fori_loop(0, key_blocks, turn, 0)
        loads[3].wait()
        loads[4].wait()

    length = lengths[0]
    count = counts[0]

    def step_pass(m):
        await_bytes(rows.at[0, 0, pl.ds(0, 4)], recv.at[m, ROWS1])
        push(rows.at[m, core, 0], rows.at[m, core, 7], ROWS2, m, along(1))
        push(rows.at[m, core, 4], rows.at[m, core, 5], ROWS2, m, along(-1))
        push(rows.at[m, core, 0, 0], rows.at[m, core, 6, 0], ROWS2, m, along(2))
        push(rows.at[m, core, 4, 1], rows.at[m, core, 6, 1], ROWS2, m, along(-2))
        push(rows.at[m, core, pl.ds(0, 5)], rows.at[m, core, pl.ds(0, 5)], ROWS_SIB, m, sibling)

    def project_half(m, i):
        block = rows[m, i].reshape(CHIPS * 2 * T, rows.shape[-1]).astype(F32)
        scaled = (block * gains[i, 0:1, :]).astype(BF16)
        return dot(scaled, w_in[i]), jnp.sum(block * block, axis=1, keepdims=True)

    def step_last_rows(m):
        await_bytes(rows.at[0, 0, pl.ds(0, 3)], recv.at[m, ROWS2])
        push(rows.at[m, core, pl.ds(5, 3)], rows.at[m, core, pl.ds(5, 3)], ROWS_SIB, m, sibling)
        pl.when(m == 0)(weights_ready)
        half_sum[m], half_sq[m] = project_half(m, core)

    def step_project(m):
        await_bytes(rows.at[0, 0], recv.at[m, ROWS_SIB])
        total, total_sq = project_half(m, 1 - core)
        total = total + half_sum[m]
        total_sq = total_sq + half_sq[m]
        part[m] = total.reshape(CHIPS, 2, T, total.shape[1]).astype(BF16)
        wide = jnp.broadcast_to(total_sq, (CHIPS * 2 * T, HEAD_DIM))
        lane = lax.broadcasted_iota(jnp.int32, wide.shape, 1)
        high = wide.astype(BF16)
        low = (wide - high.astype(F32)).astype(BF16)
        packed = jnp.where(lane == 0, high.astype(F32), jnp.where(lane == 1, low.astype(F32), 0.0))
        sq_send[m] = packed.reshape(CHIPS, 2, T, HEAD_DIM).astype(BF16)
        for dx, dy in offsets:
            for dc in range(2):
                if (dx, dy, dc) == (0, 0, 0):
                    continue
                to_chip, to_core, device = planar(dx, dy, dc)
                place = (to_chip - z + OWN + NZ) % NZ
                push(part.at[m, place, to_core], sums.at[m, dc * CHIPS + dx * NY + dy], SUMS, m, device)
                if dc == 0:
                    push(sq_send.at[m, place, to_core], sq_recv.at[m, dx * NY + dy], SQUARES, m, device)

    def step_attend(m):
        pl.when(m == 0)(prepare)
        await_bytes(sums.at[0, pl.ds(0, 15)], recv.at[m, SUMS])
        await_bytes(sq_recv.at[0, pl.ds(0, 7)], recv.at[m, SQUARES])
        place = (chip - z + OWN + NZ) % NZ
        same = part[m, place, core].astype(F32)
        squares = sq_send[m, place, core].astype(F32)
        for k in range(1, CHIPS):
            same = same + sums[m, k].astype(F32)
            squares = squares + sq_recv[m, k].astype(F32)
        other = sums[m, CHIPS].astype(F32)
        for k in range(CHIPS + 1, 2 * CHIPS):
            other = other + sums[m, k].astype(F32)
        inverse = lax.rsqrt(jnp.sum(squares, axis=1, keepdims=True) / D + EPSILON)
        same = same * inverse
        other = other * inverse
        first = jnp.where(core == 0, same, other).astype(BF16)
        second = jnp.where(core == 0, other, same).astype(BF16)
        query = jnp.concatenate(
            [g[:, h * HEAD_DIM:(h + 1) * HEAD_DIM] for g in (first, second) for h in range(half // HEAD_DIM)], axis=0)
        slots = pl.ds(pl.multiple_of(m * T, T), T)
        keys_new[slots, :] = first[:, half:]
        values_new[slots, :] = second[:, half:]

        lane_slot = lax.broadcasted_iota(jnp.int32, (TREE, lanes), 1) % T + m * T
        pick = jnp.where(lax.broadcasted_iota(jnp.int32, (TREE, lanes), 0) == lane_slot, 1.0, 0.0).astype(BF16)
        reached = dot(reach[...], pick) > 0.5
        tree_scores = jnp.where(reached, dot_nt(keys_new[...], query), LOW)
        top = jnp.max(tree_scores, axis=0, keepdims=True)
        position = lax.broadcasted_iota(jnp.int32, (key_block, lanes), 0)
        for b in range(key_blocks):
            block = dot_nt(keys[b * key_block:(b + 1) * key_block, :], query)
            block = jnp.where(position < length - b * key_block, block, LOW)
            scores[b] = block
            top = jnp.maximum(top, jnp.max(block, axis=0, keepdims=True))
        weights = jnp.exp2((tree_scores - top) * SCORE_SCALE)
        total = jnp.sum(weights, axis=0, keepdims=True)
        values_new_t = dot_nt(identity, values_new[...]).astype(BF16)
        mixed = dot(values_new_t, weights.astype(BF16))
        for b in range(key_blocks):
            weights = jnp.exp2((scores[b] - top) * SCORE_SCALE)
            total = total + jnp.sum(weights, axis=0, keepdims=True)
            mixed = mixed + dot(values_t[b], weights.astype(BF16))
        live = lax.broadcasted_iota(jnp.int32, (1, lanes), 1) % T + m * T < count
        mixed = jnp.where(live, mixed / total, 0.0).T.astype(BF16)
        for h in range(lanes // T):
            heads[m, core, chip, :, h * HEAD_DIM:(h + 1) * HEAD_DIM] = mixed[h * T:(h + 1) * T, :]
        for dx, dy in offsets:
            if (dx, dy) != (0, 0):
                push(heads.at[m, core, chip], heads.at[m, core, chip], HEADS, m, planar(dx, dy, 0)[2])

    def out_half(m, i):
        product = dot(heads[m, i].reshape(CHIPS * T, heads.shape[-1]), w_o[...]).astype(BF16)
        outp[m, :, i] = product.reshape(CHIPS, T, product.shape[1])

    def step_heads(m):
        await_bytes(heads.at[0, 0, pl.ds(0, 7)], recv.at[m, HEADS])
        push(heads.at[m, core], heads.at[m, core], HEADS_SIB, m, sibling)
        out_half(m, core)

    def step_out(m):
        await_bytes(heads.at[0, 0], recv.at[m, HEADS_SIB])
        out_half(m, 1 - core)
        push(outp.at[m, (z + 4) % NZ, 0], out1.at[m, 2, 0], OUT1, m, along(2))
        push(outp.at[m, (z + 4) % NZ, 1], out1.at[m, 2, 1], OUT1, m, along(-2))
        push(outp.at[m, (z + 3) % NZ], out1.at[m, 0], OUT1, m, along(1))
        push(outp.at[m, (z + 5) % NZ], out1.at[m, 1], OUT1, m, along(-1))
        push(outp.at[m, (z + 1) % NZ], out2.at[m, 2], OUT2, m, along(1))
        push(outp.at[m, (z + 7) % NZ], out2.at[m, 3], OUT2, m, along(-1))

    def step_merge(m):
        await_bytes(out1.at[0], recv.at[m, OUT1])
        for side, by in enumerate((2, -2)):
            both = outp[m, (z + by + NZ) % NZ].astype(F32) + out1[m, side].astype(F32)
            merged[m, side] = both.astype(BF16)
            merged[m, side, side] = (both[side] + out1[m, 2, side].astype(F32)).astype(BF16)
            push(merged.at[m, side], out2.at[m, side], OUT2, m, along(by))

    def step_finish(m):
        await_bytes(out2.at[0], recv.at[m, OUT2])
        total = outp[m, z].astype(F32)
        for k in range(4):
            total = total + out2[m, k].astype(F32)
        result = (total + rows[m, core, OWN].astype(F32)).astype(BF16)
        handed[m] = result

        @pl.when(sec == 0)
        def _():
            push(handed.at[m], rows.at[m, core, OWN], HAND, m, other_section)
        write(m).start()

    def write(m):
        return pltpu.make_async_copy(
            handed.at[m], out.at[:, pl.ds(pl.multiple_of(m * T, T), T)], out_sem.at[m])

    steps = [step_rows, step_pass, step_last_rows, step_project, step_attend,
             step_heads, step_out, step_merge, step_finish]

    def tick(t, carry):
        for k in reversed(range(len(steps))):
            since = t - PLACES[k]
            run = (since >= 0) & (since <= (BATCHES - 1) * OFFSET)
            if OFFSET > 1:
                run = run & (since % OFFSET == 0)

            @pl.when(run)
            def _(k=k, since=since):
                steps[k](since // OFFSET)
        return carry
    lax.fori_loop(0, PLACES[-1] + (BATCHES - 1) * OFFSET + 1, tick, 0)

    def drain(m, carry):
        write(m).wait()
        await_bytes(rows.at[0, 0, pl.ds(0, 4)], send.at[m, ROWS1])
        await_bytes(rows.at[0, 0, pl.ds(0, 3)], send.at[m, ROWS2])
        await_bytes(rows.at[0, 0], send.at[m, ROWS_SIB])
        await_bytes(sums.at[0, pl.ds(0, 15)], send.at[m, SUMS])
        await_bytes(sq_recv.at[0, pl.ds(0, 7)], send.at[m, SQUARES])
        await_bytes(heads.at[0, 0, pl.ds(0, 7)], send.at[m, HEADS])
        await_bytes(heads.at[0, 0], send.at[m, HEADS_SIB])
        await_bytes(out1.at[0], send.at[m, OUT1])
        await_bytes(out2.at[0], send.at[m, OUT2])

        @pl.when(sec == 0)
        def _():
            await_bytes(handed.at[0], send.at[m, HAND])
        return carry
    lax.fori_loop(0, BATCHES, drain, 0)


def body(draft_rows, norm_gain, w_query, w_keyval, w_out, kv_cache, tree_counts, cache_lengths, tree_parents):
    T, N = SLOTS, BATCHES
    feats = draft_rows.shape[1]
    width = w_query.shape[2]
    positions = kv_cache.shape[3]
    half = width // 2 + HEAD_DIM
    lanes = width // HEAD_DIM * T
    blocks = positions // KEY_BLOCK
    vmem = pl.BlockSpec(memory_space=pltpu.VMEM)
    smem = pl.BlockSpec(memory_space=pltpu.SMEM)
    anywhere = pl.BlockSpec(memory_space=pltpu.HBM)
    result = pl.pallas_call(
        kernel,
        out_shape=jax.ShapeDtypeStruct((2, TREE, feats), BF16),
        in_specs=[anywhere, vmem, anywhere, anywhere, anywhere, anywhere, anywhere, smem, smem],
        out_specs=anywhere,
        scratch_shapes=[
            pltpu.VMEM((1, TREE), jnp.int32),
            pltpu.VMEM((N, 2, NZ, 2, T, feats), BF16),
            pltpu.VMEM((2, 8, feats), F32),
            pltpu.VMEM((2, feats, half), BF16),
            pltpu.VMEM((width, feats), BF16),
            pltpu.VMEM((positions, HEAD_DIM), BF16),
            pltpu.VMEM((positions, HEAD_DIM), BF16),
            pltpu.VMEM((blocks, HEAD_DIM, KEY_BLOCK), BF16),
            pltpu.VMEM((N, CHIPS * 2 * T, half), F32),
            pltpu.VMEM((N, CHIPS * 2 * T, 1), F32),
            pltpu.VMEM((N, CHIPS, 2, T, half), BF16),
            pltpu.VMEM((N, 2 * CHIPS, T, half), BF16),
            pltpu.VMEM((N, CHIPS, 2, T, HEAD_DIM), BF16),
            pltpu.VMEM((N, CHIPS, T, HEAD_DIM), BF16),
            pltpu.VMEM((TREE, HEAD_DIM), BF16),
            pltpu.VMEM((TREE, HEAD_DIM), BF16),
            pltpu.VMEM((TREE, TREE), BF16),
            pltpu.VMEM((blocks, KEY_BLOCK, lanes), F32),
            pltpu.VMEM((N, 2, CHIPS, T, width), BF16),
            pltpu.VMEM((N, NZ, 2, T, feats), BF16),
            pltpu.VMEM((N, 3, 2, T, feats), BF16),
            pltpu.VMEM((N, 2, 2, T, feats), BF16),
            pltpu.VMEM((N, 4, 2, T, feats), BF16),
            pltpu.VMEM((N, 2, T, feats), BF16),
            pltpu.SemaphoreType.DMA((N, 10)),
            pltpu.SemaphoreType.DMA((N, 10)),
            pltpu.SemaphoreType.DMA((6,)),
            pltpu.SemaphoreType.DMA((3,)),
            pltpu.SemaphoreType.DMA((3,)),
            pltpu.SemaphoreType.DMA((N,)),
        ],
        compiler_params=pltpu.CompilerParams(
            collective_id=0, has_side_effects=True, vmem_limit_bytes=58 << 20),
        name="two_layers",
    )(
        draft_rows.reshape(2, TREE, feats), norm_gain, w_query, w_keyval, w_out, kv_cache,
        tree_parents, tree_counts, cache_lengths,
    )
    return result.reshape(1, 2 * TREE, feats)


def solution(mesh):
    placed = (
        P("tp", "req"),
        P("section", "req"),
        P("section", "req", "tp"),
        P("section", None, "req", "tp"),
        P("section", "tp", "req"),
        P("section", "req", None, None, "tp"),
        P("req"),
        P("req"),
        P("req", None),
    )
    return jax.shard_map(
        body, mesh=mesh, in_specs=placed, out_specs=P("section", "tp", "req"), check_vma=False
    )
```
